32 devices in a mesh: groups: 2 (over y), cuts: 2 (over x), row: 4 (over z), sub: 2 (over core).
Axes of the slice: x: 2, y: 2, z: 4, core: 2. Of those that a mesh axis runs over, the one named last changes fastest.
Arguments:
- hop: bfloat16 [48, 6, 128, 128], P(('groups', 'row')), parts along dimension 0, may hold values from -0.21875 to 0.21875
- pattern: int32 [48, 6], P(('groups', 'row')), parts along dimension 0, may hold values from 0 to 23, as said below
- vectors: bfloat16 [2, 6144, 512], P('cuts', ('groups', 'row'), 'sub'), parts along dimension 1, may hold values from -6 to 6
- counts: int32 [4], P(('groups', 'cuts')), parts along dimension 0, may hold values from 256 to 512, as said below
- center: float32 [4], P(('groups', 'cuts')), parts along dimension 0, may hold values from -1 to 1
- halfwidth: float32 [4], P(('groups', 'cuts')), parts along dimension 0, may hold values from 1.5 to 3
Outputs:
- margin: float32 [4, 2, 256, 512], P(('groups', 'cuts'), 'sub', 'row'), parts along dimension 0
The draws below stay inside these ranges and needn't reach their ends.
There are 2 independent parts, one for each index of `groups`. The reference program is written for one: setup_inputs(seed, part) draws one part's arguments, and reference() takes and returns one part's arrays. A program takes and returns all parts, laid end to end along the dimension named above; each array names one. Nothing has to cross between parts.
Inputs may be any that keep to these rules, and one draw needn't show every extreme that they name: `pattern`: block row i's stored blocks lie in block columns (i + o) mod 24 for 6 distinct offsets o between -3 and 3; the offsets 0, -3 and 3 appear in every block row. `counts`: at least one slice has all 512 vectors live.
All inputs are finite; a program needn't handle non-finite values.
Results may differ from the reference program's by a relative error of at most 0.00061.
Values may be sent and summed in bfloat16 or wider, within the bound.
A program may use at most 64 MiB of HBM per device.

```python
import jax
import jax.numpy as jnp

BS = 128
NNZ = 6
W = 3
NV = 512
NBR = 24
ORDER = 3072
NVH = 256
SLICES = 2


def draw_pattern(key, part):
    spare = 2 * W - 2
    candidates = jnp.concatenate([jnp.arange(-W + 1, 0, dtype=jnp.int32), jnp.arange(1, W, dtype=jnp.int32)])
    scores = jax.random.randint(key, (NBR, spare), 0, 1000, dtype=jnp.int32) * spare + jnp.arange(spare, dtype=jnp.int32)[None, :]
    chosen = jnp.argsort(scores, axis=1)[:, :NNZ - 3]
    offsets = jnp.concatenate([jnp.zeros((NBR, 1), jnp.int32), jnp.full((NBR, 1), -W, jnp.int32), jnp.full((NBR, 1), W, jnp.int32), candidates[chosen]], axis=1)
    block_rows = jnp.arange(NBR, dtype=jnp.int32)[:, None]
    return ((block_rows + offsets) % NBR).astype(jnp.int32)


def draw_counts(key, part):
    first_key = jax.random.fold_in(key, 11)
    second_key = jax.random.fold_in(key, 12)
    values = jax.random.randint(first_key, (SLICES,), NV // 2, NV + 1, dtype=jnp.int32)
    fullest = jax.random.randint(second_key, (), 0, SLICES, dtype=jnp.int32)
    return jnp.where(jnp.arange(SLICES, dtype=jnp.int32) == fullest, NV, values).astype(jnp.int32)


def levels(stream_key, dims, shards, least, high):
    loudness = 1.0
    for position, shards_of in shards:
        draws = jax.random.uniform(jax.random.fold_in(jax.random.fold_in(stream_key, 6), position), (shards_of,), jnp.float32, least / len(shards), high / len(shards))
        loudness = loudness * jnp.repeat(jnp.exp(draws), dims[position] // shards_of).reshape((-1,) + (1,) * (len(dims) - 1 - position))
    return loudness


def normal_values(key, extent, spread, reach, shards=(), kind=jnp.bfloat16):
    result = spread * jax.random.normal(key, extent, jnp.float32)
    if shards:
        result = result * levels(key, extent, shards, -0.22, 0.18)
    return jnp.clip(result, -reach, reach).astype(kind)


def setup_inputs(seed: int = 0, part: int = 0) -> dict:
    arg_keys = jax.random.split(jax.random.key(seed), 7)
    part_keys = jax.random.split(jax.random.fold_in(arg_keys[6], part), 7)
    return {
        "hop": normal_values(part_keys[0], (NBR, NNZ, BS, BS), (NNZ * BS) ** -0.5, 0.21875, ((0, 4),)),
        "pattern": draw_pattern(jax.random.fold_in(jax.random.fold_in(arg_keys[6], part), 71), part),
        "vectors": normal_values(part_keys[2], (SLICES, ORDER, NV), 1.0, 6.0, ((0, 2), (1, 4), (2, 2))),
        "counts": draw_counts(jax.random.fold_in(jax.random.fold_in(arg_keys[6], part), 71), part),
        "center": jnp.clip(jax.random.uniform(part_keys[4], (SLICES,), jnp.float32, -1.0, 1.0) * levels(part_keys[4], (SLICES,), ((0, 2),), -0.4, 0.0), -1.0, 1.0),
        "halfwidth": jnp.clip(1.5 + 1.5 * jax.random.uniform(part_keys[5], (SLICES,), jnp.float32) ** levels(part_keys[5], (SLICES,), ((0, 2),), -0.2, 0.2), 1.5, 3.0),
    }


def apply_hop(hop, pattern, field):
    blocks = field.reshape(NBR, BS, NV)
    total = jnp.zeros((NBR, BS, NV), jnp.float32)
    for k in range(NNZ):
        picked = blocks[pattern[:, k]]
        total = total + jnp.einsum("rij,rjn->rin", hop[:, k].astype(jnp.float32), picked.astype(jnp.float32))
    return total.reshape(ORDER, NV)


def reference(hop, pattern, vectors, counts, center, halfwidth):
    results = []
    for s in range(SLICES):
        live = (jnp.arange(NV, dtype=jnp.int32) < counts[s]).astype(jnp.bfloat16)
        start = vectors[s] * live[None, :]
        first_image = apply_hop(hop, pattern, start)
        step_one = ((first_image - center[s] * start.astype(jnp.float32)) / halfwidth[s]).astype(jnp.bfloat16)
        second_image = apply_hop(hop, pattern, step_one)
        filtered = (2.0 * (second_image - center[s] * step_one.astype(jnp.float32)) / halfwidth[s] - start.astype(jnp.float32)).astype(jnp.bfloat16)
        gram = jnp.dot(filtered.T, filtered, preferred_element_type=jnp.float32) / ORDER
        results.append(gram.reshape(2, NVH, NV))
    return jnp.stack(results)
```

```python
import functools

import jax
import jax.numpy as jnp
from jax import lax
from jax.experimental import pallas as pl
from jax.experimental.pallas import tpu as pltpu
from jax.sharding import PartitionSpec as P

W = 3
MESH = pl.DeviceIdType.MESH
PEAK = 32767.0
FLOOR = 1e-33


def dot(a, b):
    return jnp.dot(a, b, preferred_element_type=jnp.float32)


def kernel(
    n, rows, bs, half, nnz,
    pattern, counts, center, width, hop_hbm, vec_hbm, out,
    hop, band, ext0, ext1, acc, fil, qsend, qrecv, ssend, srecv, own,
    load_sem, h1_send, h1_recv, h2_send, h2_recv, f_send, f_recv, g_send, g_recv, c_send, c_recv,
):
    me = lax.axis_index("row")
    sub = lax.axis_index("sub")
    other = 1 - sub
    right, left = lax.rem(me + 1, n), lax.rem(me + n - 1, n)
    total_blocks = n * rows
    share = half // n
    top = W + rows

    def at(block):
        return pl.ds(block * bs, bs)

    load_v = pltpu.make_async_copy(
        vec_hbm.at[0], ext0.at[pl.ds(W * bs, rows * bs)], load_sem.at[0]
    )
    load_h = pltpu.make_async_copy(hop_hbm, hop, load_sem.at[1])
    load_v.start()
    load_h.start()

    barrier = pltpu.get_barrier_semaphore()
    for d in range(1, n):
        pl.semaphore_signal(
            barrier, inc=1, device_id={"row": lax.rem(me + d, n)}, device_id_type=MESH
        )
    pl.semaphore_signal(barrier, inc=1, device_id={"sub": other}, device_id_type=MESH)
    pl.semaphore_wait(barrier, n)

    def to_row(src, dst, send, recv, target):
        return pltpu.make_async_remote_copy(
            src_ref=src, dst_ref=dst, send_sem=send, recv_sem=recv,
            device_id={"row": target}, device_id_type=MESH,
        )

    first = []
    for j in range(W):
        up = to_row(
            vec_hbm.at[0, at(rows - 1 - j)], ext0.at[at(W - 1 - j)],
            h1_send.at[j], h1_recv.at[j], right,
        )
        down = to_row(
            vec_hbm.at[0, at(j)], ext0.at[at(top + j)],
            h1_send.at[W + j], h1_recv.at[W + j], left,
        )
        up.start()
        down.start()
        first.append((up, down))

    live = (
        lax.broadcasted_iota(jnp.int32, (1, half), 1) + sub * half < counts[0]
    )
    shift = center[0]
    inverse = 1.0 / jnp.full((1, half), width[0], jnp.float32)

    def mask(block):
        part = ext0[at(block), :]
        ext0[at(block), :] = jnp.where(live, part, jnp.zeros_like(part))

    load_h.wait()
    for i in range(rows):
        for o in range(2 * W + 1):
            want = lax.rem(me * rows + i + o - W + total_blocks, total_blocks)
            where = jnp.int32(0)
            found = jnp.int32(0)
            for k in range(nnz):
                hit = pattern[i, k] == want
                where = jnp.where(hit, k, where)
                found = jnp.where(hit, 1, found)
            block = hop[i, where]
            present = jnp.full((bs, bs), found, jnp.int32) > 0
            band[i, :, o * bs : (o + 1) * bs] = jnp.where(
                present, block.astype(jnp.float32), 0.0
            ).astype(jnp.bfloat16)

    load_v.wait()
    for i in range(rows):
        mask(W + i)

    def piece(i, low, high, ext):
        return dot(
            band[i, :, (low - i) * bs : (high - i) * bs], ext[low * bs : high * bs, :]
        )

    def local(i, ext):
        return piece(i, max(i, W), min(i + 2 * W + 1, top), ext)

    for i in range(rows):
        acc[at(i), :] = local(i, ext0)

    second = []

    def finish_one(i):
        start = ext0[at(W + i), :].astype(jnp.float32)
        ext1[at(W + i), :] = ((acc[at(i), :] - shift * start) * inverse).astype(
            jnp.bfloat16
        )

    for j in range(W):
        up, down = first[j]
        low, high = W - 1 - j, rows - W + j
        up.wait_recv()
        mask(low)
        acc[at(low), :] += piece(low, low, W, ext0)
        finish_one(low)
        go_left = to_row(
            ext1.at[at(W + low)], ext1.at[at(top + low)],
            h2_send.at[j], h2_recv.at[j], left,
        )
        go_left.start()
        down.wait_recv()
        mask(top + j)
        acc[at(high), :] += piece(high, top, top + j + 1, ext0)
        finish_one(high)
        go_right = to_row(
            ext1.at[at(W + high)], ext1.at[at(j)],
            h2_send.at[W + j], h2_recv.at[W + j], right,
        )
        go_right.start()
        second.append((go_left, go_right))

    for i in range(rows):
        acc[at(i), :] = local(i, ext1)

    for j in range(W):
        go_left, go_right = second[j]
        go_right.wait_recv()
        for i in range(j + 1):
            acc[at(i), :] += piece(i, j, j + 1, ext1)
        go_left.wait_recv()
        block = top + W - 1 - j
        for i in range(block - 2 * W, rows):
            acc[at(i), :] += piece(i, block, block + 1, ext1)

    sides = []
    for i in range(rows):
        start = ext0[at(W + i), :].astype(jnp.float32)
        one = ext1[at(W + i), :].astype(jnp.float32)
        fil[0, at(i), :] = (
            2.0 * (acc[at(i), :] - shift * one) * inverse - start
        ).astype(jnp.bfloat16)
        side = pltpu.make_async_remote_copy(
            src_ref=fil.at[0, at(i)], dst_ref=fil.at[1, at(i)],
            send_sem=f_send.at[i], recv_sem=f_recv.at[i],
            device_id={"sub": other}, device_id_type=MESH,
        )
        side.start()
        sides.append(side)

    mine = fil[0].T
    sends = []
    for p in range(2):
        if p:
            for side in sides:
                side.wait_recv()
        term = dot(mine, fil[p])
        own[p] = term.reshape(n, share, half)
        for t in range(n):
            part = term[t * share : (t + 1) * share, :]
            peak = jnp.maximum(jnp.max(jnp.abs(part), axis=0, keepdims=True), FLOOR)
            qsend[p, t] = jnp.round(part * (PEAK / peak)).astype(jnp.int32).astype(qsend.dtype)
            ssend[p, t] = peak * (1.0 / PEAK)
        for d in range(1, n):
            target = lax.rem(me + d, n)
            values = to_row(
                qsend.at[p, target], qrecv.at[p, d - 1],
                g_send.at[p, d - 1], g_recv.at[p, d - 1], target,
            )
            scales = to_row(
                ssend.at[p, target], srecv.at[p, d - 1],
                c_send.at[p, d - 1], c_recv.at[p, d - 1], target,
            )
            scales.start()
            values.start()
            sends.append((p, d, values, scales))

    scale = 1.0 / (total_blocks * bs)
    for p in range(2):
        total = own[p, me]
        for q, d, values, scales in sends:
            if q == p:
                scales.wait_recv()
                values.wait_recv()
                total = total + qrecv[p, d - 1].astype(jnp.int32).astype(
                    jnp.float32
                ) * srecv[p, d - 1]
        column = sub if p == 0 else other
        out[:, pl.ds(pl.multiple_of(column * half, half), half)] = total * scale

    for pair in first + second:
        for copy in pair:
            copy.wait_send()
    for side in sides:
        side.wait_send()
    for _, _, values, scales in sends:
        values.wait_send()
        scales.wait_send()


def body(hop, pattern, vectors, counts, center, halfwidth):
    rows, nnz, bs, _ = hop.shape
    half = vectors.shape[2]
    n = lax.axis_size("row")
    share = half // n
    code = jnp.int16 if share % 16 == 0 else jnp.int32
    dma = pltpu.SemaphoreType.DMA
    smem = pl.BlockSpec(memory_space=pltpu.SMEM)
    hbm = pl.BlockSpec(memory_space=pl.ANY)
    flops = 2 * rows * bs * half * (2 * (2 * W + 1) * bs + 2 * half)
    margin = pl.pallas_call(
        functools.partial(kernel, n, rows, bs, half, nnz),
        out_shape=jax.ShapeDtypeStruct((share, 2 * half), jnp.float32),
        in_specs=[smem, smem, smem, smem, hbm, hbm],
        out_specs=pl.BlockSpec(memory_space=pltpu.VMEM),
        scratch_shapes=[
            pltpu.VMEM(hop.shape, jnp.bfloat16),
            pltpu.VMEM((rows, bs, (2 * W + 1) * bs), jnp.bfloat16),
            pltpu.VMEM(((rows + 2 * W) * bs, half), jnp.bfloat16),
            pltpu.VMEM(((rows + 2 * W) * bs, half), jnp.bfloat16),
            pltpu.VMEM((rows * bs, half), jnp.float32),
            pltpu.VMEM((2, rows * bs, half), jnp.bfloat16),
            pltpu.VMEM((2, n, share, half), code),
            pltpu.VMEM((2, n - 1, share, half), code),
            pltpu.VMEM((2, n, 1, half), jnp.float32),
            pltpu.VMEM((2, n - 1, 1, half), jnp.float32),
            pltpu.VMEM((2, n, share, half), jnp.float32),
            dma((2,)),
            dma((2 * W,)), dma((2 * W,)), dma((2 * W,)), dma((2 * W,)),
            dma((rows,)), dma((rows,)),
            dma((2, n - 1)), dma((2, n - 1)), dma((2, n - 1)), dma((2, n - 1)),
        ],
        compiler_params=pltpu.CompilerParams(
            collective_id=0, has_side_effects=True, vmem_limit_bytes=40 * 2**20
        ),
        cost_estimate=pl.CostEstimate(
            flops=flops, bytes_accessed=2 * (hop.size + vectors.size), transcendentals=0
        ),
    )(pattern, counts, center, halfwidth, hop, vectors)
    return margin.reshape(1, 1, share, 2 * half)


def solution(mesh):
    in_specs = (
        P(("groups", "row"), None, None, None),
        P(("groups", "row"), None),
        P("cuts", ("groups", "row"), "sub"),
        P(("groups", "cuts")),
        P(("groups", "cuts")),
        P(("groups", "cuts")),
    )
    out_specs = P(("groups", "cuts"), "sub", "row", None)
    return jax.shard_map(body, mesh=mesh, in_specs=in_specs, out_specs=out_specs, check_vma=False)
```

```python
import functools

import jax
import jax.numpy as jnp
from jax import lax
from jax.experimental import pallas as pl
from jax.experimental.pallas import tpu as pltpu
from jax.sharding import PartitionSpec as P

W = 3
MESH = pl.DeviceIdType.MESH
PEAK = 32767.0
FLOOR = 1e-33


def dot(a, b):
    return jnp.dot(a, b, preferred_element_type=jnp.float32)


def kernel(
    n, rows, bs, half, nnz,
    pattern_hbm, counts_hbm, center_hbm, width_hbm, hop_hbm, vec_hbm, out,
    pattern, counts, center, width,
    hop, band, ext0, ext1, acc, fil, qsend, qrecv, ssend, srecv, own,
    load_sem, h1_send, h1_recv, h2_send, h2_recv, f_send, f_recv, g_send, g_recv, c_send, c_recv,
):
    me = lax.axis_index("row")
    sub = lax.axis_index("sub")
    other = 1 - sub
    right, left = lax.rem(me + 1, n), lax.rem(me + n - 1, n)
    total_blocks = n * rows
    share = half // n
    top = W + rows

    def at(block):
        return pl.ds(block * bs, bs)

    load_v = pltpu.make_async_copy(
        vec_hbm.at[0], ext0.at[pl.ds(W * bs, rows * bs)], load_sem.at[0]
    )
    load_h = pltpu.make_async_copy(hop_hbm, hop, load_sem.at[1])
    small = [
        pltpu.make_async_copy(source, here, load_sem.at[2 + i])
        for i, (source, here) in enumerate(
            (
                (pattern_hbm, pattern), (counts_hbm, counts),
                (center_hbm, center), (width_hbm, width),
            )
        )
    ]
    for copy in small:
        copy.start()
    load_v.start()
    load_h.start()

    barrier = pltpu.get_barrier_semaphore()
    for d in range(1, n):
        pl.semaphore_signal(
            barrier, inc=1, device_id={"row": lax.rem(me + d, n)}, device_id_type=MESH
        )
    pl.semaphore_signal(barrier, inc=1, device_id={"sub": other}, device_id_type=MESH)
    pl.semaphore_wait(barrier, n)

    def to_row(src, dst, send, recv, target):
        return pltpu.make_async_remote_copy(
            src_ref=src, dst_ref=dst, send_sem=send, recv_sem=recv,
            device_id={"row": target}, device_id_type=MESH,
        )

    first = []
    for j in range(W):
        up = to_row(
            vec_hbm.at[0, at(rows - 1 - j)], ext0.at[at(W - 1 - j)],
            h1_send.at[j], h1_recv.at[j], right,
        )
        down = to_row(
            vec_hbm.at[0, at(j)], ext0.at[at(top + j)],
            h1_send.at[W + j], h1_recv.at[W + j], left,
        )
        up.start()
        down.start()
        first.append((up, down))

    for copy in small:
        copy.wait()
    live = (
        lax.broadcasted_iota(jnp.int32, (1, half), 1) + sub * half < counts[0]
    )
    shift = center[0]
    inverse = 1.0 / jnp.full((1, half), width[0], jnp.float32)

    def mask(block):
        part = ext0[at(block), :]
        ext0[at(block), :] = jnp.where(live, part, jnp.zeros_like(part))

    load_h.wait()
    for i in range(rows):
        for o in range(2 * W + 1):
            want = lax.rem(me * rows + i + o - W + total_blocks, total_blocks)
            where = jnp.int32(0)
            found = jnp.int32(0)
            for k in range(nnz):
                hit = pattern[i, k] == want
                where = jnp.where(hit, k, where)
                found = jnp.where(hit, 1, found)
            block = hop[i, where]
            present = jnp.full((bs, bs), found, jnp.int32) > 0
            band[i, :, o * bs : (o + 1) * bs] = jnp.where(
                present, block.astype(jnp.float32), 0.0
            ).astype(jnp.bfloat16)

    load_v.wait()
    for i in range(rows):
        mask(W + i)

    def piece(i, low, high, ext):
        return dot(
            band[i, :, (low - i) * bs : (high - i) * bs], ext[low * bs : high * bs, :]
        )

    def local(i, ext):
        return piece(i, max(i, W), min(i + 2 * W + 1, top), ext)

    for i in range(rows):
        acc[at(i), :] = local(i, ext0)

    second = []

    def finish_one(i):
        start = ext0[at(W + i), :].astype(jnp.float32)
        ext1[at(W + i), :] = ((acc[at(i), :] - shift * start) * inverse).astype(
            jnp.bfloat16
        )

    for j in range(W):
        up, down = first[j]
        low, high = W - 1 - j, rows - W + j
        up.wait_recv()
        mask(low)
        acc[at(low), :] += piece(low, low, W, ext0)
        finish_one(low)
        go_left = to_row(
            ext1.at[at(W + low)], ext1.at[at(top + low)],
            h2_send.at[j], h2_recv.at[j], left,
        )
        go_left.start()
        down.wait_recv()
        mask(top + j)
        acc[at(high), :] += piece(high, top, top + j + 1, ext0)
        finish_one(high)
        go_right = to_row(
            ext1.at[at(W + high)], ext1.at[at(j)],
            h2_send.at[W + j], h2_recv.at[W + j], right,
        )
        go_right.start()
        second.append((go_left, go_right))

    for i in range(rows):
        acc[at(i), :] = local(i, ext1)

    for j in range(W):
        go_left, go_right = second[j]
        go_right.wait_recv()
        for i in range(j + 1):
            acc[at(i), :] += piece(i, j, j + 1, ext1)
        go_left.wait_recv()
        block = top + W - 1 - j
        for i in range(block - 2 * W, rows):
            acc[at(i), :] += piece(i, block, block + 1, ext1)

    sides = []
    for i in range(rows):
        start = ext0[at(W + i), :].astype(jnp.float32)
        one = ext1[at(W + i), :].astype(jnp.float32)
        fil[0, at(i), :] = (
            2.0 * (acc[at(i), :] - shift * one) * inverse - start
        ).astype(jnp.bfloat16)
        side = pltpu.make_async_remote_copy(
            src_ref=fil.at[0, at(i)], dst_ref=fil.at[1, at(i)],
            send_sem=f_send.at[i], recv_sem=f_recv.at[i],
            device_id={"sub": other}, device_id_type=MESH,
        )
        side.start()
        sides.append(side)

    mine = fil[0].T
    sends = []
    for p in range(2):
        if p:
            for side in sides:
                side.wait_recv()
        term = dot(mine, fil[p])
        own[p] = term.reshape(n, share, half)
        for t in range(n):
            part = term[t * share : (t + 1) * share, :]
            peak = jnp.maximum(jnp.max(jnp.abs(part), axis=0, keepdims=True), FLOOR)
            qsend[p, t] = jnp.round(part * (PEAK / peak)).astype(jnp.int32).astype(qsend.dtype)
            ssend[p, t] = peak * (1.0 / PEAK)
        for d in range(1, n):
            target = lax.rem(me + d, n)
            values = to_row(
                qsend.at[p, target], qrecv.at[p, d - 1],
                g_send.at[p, d - 1], g_recv.at[p, d - 1], target,
            )
            scales = to_row(
                ssend.at[p, target], srecv.at[p, d - 1],
                c_send.at[p, d - 1], c_recv.at[p, d - 1], target,
            )
            scales.start()
            values.start()
            sends.append((p, d, values, scales))

    scale = 1.0 / (total_blocks * bs)
    for p in range(2):
        total = own[p, me]
        for q, d, values, scales in sends:
            if q == p:
                scales.wait_recv()
                values.wait_recv()
                total = total + qrecv[p, d - 1].astype(jnp.int32).astype(
                    jnp.float32
                ) * srecv[p, d - 1]
        column = sub if p == 0 else other
        out[:, pl.ds(pl.multiple_of(column * half, half), half)] = total * scale

    for pair in first + second:
        for copy in pair:
            copy.wait_send()
    for side in sides:
        side.wait_send()
    for _, _, values, scales in sends:
        values.wait_send()
        scales.wait_send()


def body(hop, pattern, vectors, counts, center, halfwidth):
    rows, nnz, bs, _ = hop.shape
    half = vectors.shape[2]
    n = lax.axis_size("row")
    share = half // n
    code = jnp.int16 if share % 16 == 0 else jnp.int32
    dma = pltpu.SemaphoreType.DMA
    hbm = pl.BlockSpec(memory_space=pltpu.HBM)
    flops = 2 * rows * bs * half * (2 * (2 * W + 1) * bs + 2 * half)
    margin = pl.pallas_call(
        functools.partial(kernel, n, rows, bs, half, nnz),
        out_shape=jax.ShapeDtypeStruct((share, 2 * half), jnp.float32),
        in_specs=[hbm] * 6,
        out_specs=pl.BlockSpec(memory_space=pltpu.VMEM),
        scratch_shapes=[
            pltpu.SMEM(pattern.shape, jnp.int32),
            pltpu.SMEM(counts.shape, jnp.int32),
            pltpu.SMEM(center.shape, jnp.float32),
            pltpu.SMEM(halfwidth.shape, jnp.float32),
            pltpu.VMEM(hop.shape, jnp.bfloat16),
            pltpu.VMEM((rows, bs, (2 * W + 1) * bs), jnp.bfloat16),
            pltpu.VMEM(((rows + 2 * W) * bs, half), jnp.bfloat16),
            pltpu.VMEM(((rows + 2 * W) * bs, half), jnp.bfloat16),
            pltpu.VMEM((rows * bs, half), jnp.float32),
            pltpu.VMEM((2, rows * bs, half), jnp.bfloat16),
            pltpu.VMEM((2, n, share, half), code),
            pltpu.VMEM((2, n - 1, share, half), code),
            pltpu.VMEM((2, n, 1, half), jnp.float32),
            pltpu.VMEM((2, n - 1, 1, half), jnp.float32),
            pltpu.VMEM((2, n, share, half), jnp.float32),
            dma((6,)),
            dma((2 * W,)), dma((2 * W,)), dma((2 * W,)), dma((2 * W,)),
            dma((rows,)), dma((rows,)),
            dma((2, n - 1)), dma((2, n - 1)), dma((2, n - 1)), dma((2, n - 1)),
        ],
        compiler_params=pltpu.CompilerParams(
            collective_id=0, has_side_effects=True, vmem_limit_bytes=62 * 2**20
        ),
        cost_estimate=pl.CostEstimate(
            flops=flops, bytes_accessed=2 * (hop.size + vectors.size), transcendentals=0
        ),
    )(pattern, counts, center, halfwidth, hop, vectors)
    return margin.reshape(1, 1, share, 2 * half)


def solution(mesh):
    in_specs = (
        P(("groups", "row"), None, None, None),
        P(("groups", "row"), None),
        P("cuts", ("groups", "row"), "sub"),
        P(("groups", "cuts")),
        P(("groups", "cuts")),
        P(("groups", "cuts")),
    )
    out_specs = P(("groups", "cuts"), "sub", "row", None)
    return jax.shard_map(body, mesh=mesh, in_specs=in_specs, out_specs=out_specs, check_vma=False)
```

```python
import functools

import jax
import jax.numpy as jnp
from jax import lax
from jax.experimental import pallas as pl
from jax.experimental.pallas import tpu as pltpu
from jax.sharding import PartitionSpec as P

W = 3
MESH = pl.DeviceIdType.MESH
PEAK = 32767.0
FLOOR = 1e-33


def dot(a, b):
    return jnp.dot(a, b, preferred_element_type=jnp.float32)


def kernel(
    n, rows, bs, half, nnz,
    pattern_hbm, counts_hbm, center_hbm, width_hbm, hop_hbm, vec_hbm, out,
    pattern, counts, center, width,
    hop, band, ext0, ext1, acc, fil, qsend, qrecv, ssend, srecv, own,
    load_sem, h1_send, h1_recv, h2_send, h2_recv, f_send, f_recv, g_send, g_recv, c_send, c_recv,
):
    me = lax.axis_index("row")
    sub = lax.axis_index("sub")
    other = 1 - sub
    right, left = lax.rem(me + 1, n), lax.rem(me + n - 1, n)
    total_blocks = n * rows
    share = half // n
    top = W + rows

    def at(block):
        return pl.ds(block * bs, bs)

    load_v = pltpu.make_async_copy(
        vec_hbm.at[0], ext0.at[pl.ds(W * bs, rows * bs)], load_sem.at[0]
    )
    load_h = pltpu.make_async_copy(hop_hbm, hop, load_sem.at[1])
    small = [
        pltpu.make_async_copy(source, here, load_sem.at[2 + i])
        for i, (source, here) in enumerate(
            (
                (pattern_hbm, pattern), (counts_hbm, counts),
                (center_hbm, center), (width_hbm, width),
            )
        )
    ]
    for copy in small:
        copy.start()
    load_v.start()
    load_h.start()

    barrier = pltpu.get_barrier_semaphore()
    for d in range(1, n):
        pl.semaphore_signal(
            barrier, inc=1, device_id={"row": lax.rem(me + d, n)}, device_id_type=MESH
        )
    pl.semaphore_signal(barrier, inc=1, device_id={"sub": other}, device_id_type=MESH)
    pl.semaphore_wait(barrier, n)

    def to_row(src, dst, send, recv, target):
        return pltpu.make_async_remote_copy(
            src_ref=src, dst_ref=dst, send_sem=send, recv_sem=recv,
            device_id={"row": target}, device_id_type=MESH,
        )

    first = []
    for j in range(W):
        up = to_row(
            vec_hbm.at[0, at(rows - 1 - j)], ext0.at[at(W - 1 - j)],
            h1_send.at[j], h1_recv.at[j], right,
        )
        down = to_row(
            vec_hbm.at[0, at(j)], ext0.at[at(top + j)],
            h1_send.at[W + j], h1_recv.at[W + j], left,
        )
        up.start()
        down.start()
        first.append((up, down))

    for copy in small:
        copy.wait()
    live = (
        lax.broadcasted_iota(jnp.int32, (1, half), 1) + sub * half < counts[0]
    )
    shift = center[0]
    inverse = 1.0 / jnp.full((1, half), width[0], jnp.float32)

    def mask(block):
        part = ext0[at(block), :]
        ext0[at(block), :] = jnp.where(live, part, jnp.zeros_like(part))

    load_h.wait()
    for i in range(rows):
        for o in range(2 * W + 1):
            want = lax.rem(me * rows + i + o - W + total_blocks, total_blocks)
            where = jnp.int32(0)
            found = jnp.int32(0)
            for k in range(nnz):
                hit = pattern[i, k] == want
                where = jnp.where(hit, k, where)
                found = jnp.where(hit, 1, found)
            block = hop[i, where]
            present = jnp.full((bs, bs), found, jnp.int32) > 0
            band[i, :, o * bs : (o + 1) * bs] = jnp.where(
                present, block.astype(jnp.float32), 0.0
            ).astype(jnp.bfloat16)

    load_v.wait()
    for i in range(rows):
        mask(W + i)

    def piece(i, low, high, ext):
        return dot(
            band[i, :, (low - i) * bs : (high - i) * bs], ext[low * bs : high * bs, :]
        )

    def local(i, ext):
        return piece(i, max(i, W), min(i + 2 * W + 1, top), ext)

    for i in range(rows):
        acc[at(i), :] = local(i, ext0)

    second = []

    def finish_one(i):
        start = ext0[at(W + i), :].astype(jnp.float32)
        ext1[at(W + i), :] = ((acc[at(i), :] - shift * start) * inverse).astype(
            jnp.bfloat16
        )

    for j in range(W):
        up, down = first[j]
        low, high = W - 1 - j, rows - W + j
        up.wait_recv()
        mask(low)
        acc[at(low), :] += piece(low, low, W, ext0)
        finish_one(low)
        go_left = to_row(
            ext1.at[at(W + low)], ext1.at[at(top + low)],
            h2_send.at[j], h2_recv.at[j], left,
        )
        go_left.start()
        down.wait_recv()
        mask(top + j)
        acc[at(high), :] += piece(high, top, top + j + 1, ext0)
        finish_one(high)
        go_right = to_row(
            ext1.at[at(W + high)], ext1.at[at(j)],
            h2_send.at[W + j], h2_recv.at[W + j], right,
        )
        go_right.start()
        second.append((go_left, go_right))

    for i in range(rows):
        acc[at(i), :] = local(i, ext1)

    for j in range(W):
        go_left, go_right = second[j]
        go_right.wait_recv()
        for i in range(j + 1):
            acc[at(i), :] += piece(i, j, j + 1, ext1)
        go_left.wait_recv()
        block = top + W - 1 - j
        for i in range(block - 2 * W, rows):
            acc[at(i), :] += piece(i, block, block + 1, ext1)

    sides = []
    for i in range(rows):
        start = ext0[at(W + i), :].astype(jnp.float32)
        one = ext1[at(W + i), :].astype(jnp.float32)
        fil[0, at(i), :] = (
            2.0 * (acc[at(i), :] - shift * one) * inverse - start
        ).astype(jnp.bfloat16)
        side = pltpu.make_async_remote_copy(
            src_ref=fil.at[0, at(i)], dst_ref=fil.at[1, at(i)],
            send_sem=f_send.at[i], recv_sem=f_recv.at[i],
            device_id={"sub": other}, device_id_type=MESH,
        )
        side.start()
        sides.append(side)

    mine = fil[0].T
    sends = []
    for p in range(2):
        if p:
            for side in sides:
                side.wait_recv()
        term = dot(mine, fil[p])
        own[p] = term.reshape(n, share, half)
        for t in range(n):
            part = term[t * share : (t + 1) * share, :]
            peak = jnp.maximum(jnp.max(jnp.abs(part), axis=0, keepdims=True), FLOOR)
            qsend[p, t] = jnp.round(part * (PEAK / peak)).astype(jnp.int32).astype(qsend.dtype)
            ssend[p, t] = peak * (1.0 / PEAK)
        for d in range(1, n):
            target = lax.rem(me + d, n)
            values = to_row(
                qsend.at[p, target], qrecv.at[p, d - 1],
                g_send.at[p, d - 1], g_recv.at[p, d - 1], target,
            )
            scales = to_row(
                ssend.at[p, target], srecv.at[p, d - 1],
                c_send.at[p, d - 1], c_recv.at[p, d - 1], target,
            )
            scales.start()
            values.start()
            sends.append((p, d, values, scales))

    scale = 1.0 / (total_blocks * bs)
    for p in range(2):
        total = own[p, me]
        for q, d, values, scales in sends:
            if q == p:
                scales.wait_recv()
                values.wait_recv()
                total = total + qrecv[p, d - 1].astype(jnp.int32).astype(
                    jnp.float32
                ) * srecv[p, d - 1]
        column = sub if p == 0 else other
        out[:, pl.ds(pl.multiple_of(column * half, half), half)] = total * scale

    for pair in first + second:
        for copy in pair:
            copy.wait_send()
    for side in sides:
        side.wait_send()
    for _, _, values, scales in sends:
        values.wait_send()
        scales.wait_send()


def body(hop, pattern, vectors, counts, center, halfwidth):
    rows, nnz, bs, _ = hop.shape
    half = vectors.shape[2]
    n = lax.axis_size("row")
    share = half // n
    code = jnp.int16 if share % 16 == 0 else jnp.int32
    dma = pltpu.SemaphoreType.DMA
    hbm = pl.BlockSpec(memory_space=pltpu.HBM)
    flops = 2 * rows * bs * half * (2 * (2 * W + 1) * bs + 2 * half)
    hop, pattern, vectors = (
        pltpu.with_memory_space_constraint(x, pltpu.HBM) for x in (hop, pattern, vectors)
    )
    margin = pl.pallas_call(
        functools.partial(kernel, n, rows, bs, half, nnz),
        out_shape=jax.ShapeDtypeStruct((share, 2 * half), jnp.float32),
        in_specs=[hbm] * 6,
        out_specs=pl.BlockSpec(memory_space=pltpu.VMEM),
        scratch_shapes=[
            pltpu.SMEM(pattern.shape, jnp.int32),
            pltpu.SMEM(counts.shape, jnp.int32),
            pltpu.SMEM(center.shape, jnp.float32),
            pltpu.SMEM(halfwidth.shape, jnp.float32),
            pltpu.VMEM(hop.shape, jnp.bfloat16),
            pltpu.VMEM((rows, bs, (2 * W + 1) * bs), jnp.bfloat16),
            pltpu.VMEM(((rows + 2 * W) * bs, half), jnp.bfloat16),
            pltpu.VMEM(((rows + 2 * W) * bs, half), jnp.bfloat16),
            pltpu.VMEM((rows * bs, half), jnp.float32),
            pltpu.VMEM((2, rows * bs, half), jnp.bfloat16),
            pltpu.VMEM((2, n, share, half), code),
            pltpu.VMEM((2, n - 1, share, half), code),
            pltpu.VMEM((2, n, 1, half), jnp.float32),
            pltpu.VMEM((2, n - 1, 1, half), jnp.float32),
            pltpu.VMEM((2, n, share, half), jnp.float32),
            dma((6,)),
            dma((2 * W,)), dma((2 * W,)), dma((2 * W,)), dma((2 * W,)),
            dma((rows,)), dma((rows,)),
            dma((2, n - 1)), dma((2, n - 1)), dma((2, n - 1)), dma((2, n - 1)),
        ],
        compiler_params=pltpu.CompilerParams(
            collective_id=0, has_side_effects=True, vmem_limit_bytes=40 * 2**20
        ),
        cost_estimate=pl.CostEstimate(
            flops=flops, bytes_accessed=2 * (hop.size + vectors.size), transcendentals=0
        ),
    )(pattern, counts, center, halfwidth, hop, vectors)
    return margin.reshape(1, 1, share, 2 * half)


def solution(mesh):
    in_specs = (
        P(("groups", "row"), None, None, None),
        P(("groups", "row"), None),
        P("cuts", ("groups", "row"), "sub"),
        P(("groups", "cuts")),
        P(("groups", "cuts")),
        P(("groups", "cuts")),
    )
    out_specs = P(("groups", "cuts"), "sub", "row", None)
    return jax.shard_map(body, mesh=mesh, in_specs=in_specs, out_specs=out_specs, check_vma=False)
```
